32 devices in a mesh: case: 2 (over y), blk: 4 (over z), split: 2 (over x), sub: 2 (over core).
Axes of the slice: x: 2, y: 2, z: 4, core: 2. Of those that a mesh axis runs over, the one named last changes fastest.
Arguments:
- cell_series: bfloat16 [32768, 4, 512], P(('case', 'blk', 'split', 'sub')), parts along dimension 0, may hold values from -6 to 6
- cell_count: int32 [32], P(('case', 'blk', 'split', 'sub')), parts along dimension 0, may hold values from 768 to 1024, as said below
- cell_target: int32 [32768], P(('case', 'blk', 'split', 'sub')), parts along dimension 0, may hold values from 0 to 2047, as said below
- surface: float32 [4, 8192], P(None, ('case', 'blk', 'split', 'sub')), parts along dimension 1, may hold values from -8.5 to 16.5, as said below
- observers: float32 [3, 1024], P(None, 'case'), parts along dimension 1, may hold values from -45 to 53, as said below
Outputs:
- pressure: float32 [1024, 2, 8], P(('case', 'blk')), parts along dimension 0
The draws below stay inside these ranges and needn't reach their ends.
There are 2 independent parts, one for each index of `case`. The reference program is written for one: setup_inputs(seed, part) draws one part's arguments, and reference() takes and returns one part's arrays. A program takes and returns all parts, laid end to end along the dimension named above; each array names one. Nothing has to cross between parts.
Inputs may be any that keep to these rules, and one draw needn't show every extreme that they name: Cells i of a device with i < cell_count are live. `cell_target`: an entry t names local surface point t mod 256 of the device whose index along blk+split is t // 256 and whose sub index is the cell's. Among the rows of one device no such owner is named more than 192 times; in every device one owner is named by exactly 192 live rows, the same owner for all devices of one sub index. Every surface point lies within 8.5 of the point (8, 0, 0); panel areas are positive. `observers`: every observer lies 18 or more from the point (8, 0, 0).
All inputs are finite; a program needn't handle non-finite values.
Results may differ from the reference program's by a relative error of at most 0.0027.
Values may be sent and summed in bfloat16 or wider, within the bound.
A program may use at most 64 MiB of HBM per device.

```python
import math
import jax
import jax.numpy as jnp
from jax import lax

NT = 512
NF = 8
R_DEV = 1024
P_DEV = 256
OBS_BLK = 128
CAP = 192
ROWS = 16384
NPTS = 4096
NOBS = 512
N_BLK = 4
N_SPLIT = 2
N_SUB = 2


def draw_cell_count(key, part):
    devices = N_BLK * N_SPLIT * N_SUB
    key_draw, key_pick = jax.random.split(jax.random.fold_in(key, 7))
    counts = jax.random.randint(key_draw, (devices,), 3 * R_DEV // 4, R_DEV + 1)
    chosen = jax.random.permutation(key_pick, devices)
    counts = counts.at[chosen[0]].set(R_DEV).at[chosen[1]].set(3 * R_DEV // 4)
    return counts.astype(jnp.int32)


def draw_cell_target(key, part):
    source_groups = N_BLK * N_SPLIT
    devices = source_groups * N_SUB
    live_least = 3 * R_DEV // 4
    key_hot, key_device = jax.random.split(jax.random.fold_in(key, 11))
    hot_owner = jax.random.randint(key_hot, (N_SUB,), 0, source_groups)
    device_keys = jax.random.split(key_device, devices)
    device_hot = hot_owner[jnp.arange(devices) % N_SUB]

    def one_device(device_key, hot_index):
        key_position, random_seed_rest, key_point = jax.random.split(device_key, 3)
        hot_rows = jax.random.permutation(key_position, live_least)[:CAP]
        flagged = jnp.zeros((R_DEV,), jnp.int32).at[hot_rows].set(1)
        remaining_sources = jnp.arange((source_groups - 1) * CAP, dtype=jnp.int32) // CAP
        remaining_sources = remaining_sources + (remaining_sources >= hot_index).astype(jnp.int32)
        remaining_sources = jax.random.permutation(random_seed_rest, remaining_sources)
        sorted_ranking = jnp.clip(jnp.cumsum(1 - flagged) - 1, 0, (source_groups - 1) * CAP - 1)
        owner_index = jnp.where(flagged == 1, hot_index, remaining_sources[sorted_ranking])
        point_index = jax.random.randint(key_point, (R_DEV,), 0, P_DEV)
        first_low = jnp.argmax((owner_index == 0).astype(jnp.int32))
        first_high = jnp.argmax((owner_index == source_groups - 1).astype(jnp.int32))
        point_index = point_index.at[first_low].set(0).at[first_high].set(P_DEV - 1)
        return owner_index * P_DEV + point_index
    return jax.vmap(one_device)(device_keys, device_hot).reshape(ROWS).astype(jnp.int32)


def draw_surface(key, part):
    key_list = jax.random.split(jax.random.fold_in(key, 3), 4)
    fraction = jax.random.uniform(key_list[0], (NPTS,), jnp.float32, 0.0, 1.0)
    distance = 8.4 * jnp.cbrt(fraction)
    cos_polar = jax.random.uniform(key_list[1], (NPTS,), jnp.float32, -1.0, 1.0)
    sin_polar = jnp.sqrt(jnp.maximum(1.0 - cos_polar * cos_polar, 0.0))
    azimuth = jax.random.uniform(key_list[2], (NPTS,), jnp.float32, -math.pi, math.pi)
    lowest, highest = (math.log(0.5), math.log(2.0))
    panel_area = jnp.exp(jax.random.uniform(key_list[3], (NPTS,), jnp.float32, lowest, highest))
    axial = 8.0 + distance * cos_polar
    sideways = distance * sin_polar
    return jnp.stack([axial, sideways * jnp.cos(azimuth), sideways * jnp.sin(azimuth), panel_area]).astype(jnp.float32)


def draw_observers(key, part):
    key_list = jax.random.split(jax.random.fold_in(key, 5), 3)
    degree = math.pi / 180.0
    polar = jax.random.uniform(key_list[0], (NOBS,), jnp.float32, 20.0 * degree, 160.0 * degree)
    distance = jax.random.uniform(key_list[1], (NOBS,), jnp.float32, 20.0, 40.0)
    azimuth = jax.random.uniform(key_list[2], (NOBS,), jnp.float32, -math.pi, math.pi)
    axial = 8.0 + distance * jnp.cos(polar)
    sideways = distance * jnp.sin(polar)
    return jnp.stack([axial, sideways * jnp.cos(azimuth), sideways * jnp.sin(azimuth)]).astype(jnp.float32)


def levels(own_key, shape, shards, smallest, high):
    factor_of, own = 1.0, jax.random.fold_in(own_key, 6)
    for axis_at, shards_of in shards:
        heights = jnp.exp(jax.random.uniform(jax.random.fold_in(own, axis_at), (shards_of,), jnp.float32, smallest / len(shards), high / len(shards)))
        factor_of = factor_of * jnp.repeat(heights, shape[axis_at] // shards_of).reshape([-1 if axis == axis_at else 1 for axis in range(len(shape))])
    return factor_of


def noise(rng, extent, width, most, cuts=(), kind=jnp.bfloat16):
    values = jax.random.normal(rng, extent, jnp.float32) * width
    if len(cuts) > 0:
        values = levels(rng, extent, cuts, -0.22, 0.18) * values
    return jnp.clip(values, min=-most, max=most).astype(kind)


def setup_inputs(seed: int = 0, part: int = 0) -> dict:
    keys = jax.random.split(jax.random.key(seed), 6)
    own_keys = jax.random.split(jax.random.fold_in(keys[5], part), 6)
    return {
        "cell_series": noise(own_keys[0], (ROWS, 4, NT), 1.0, 6.0, ((0, 16),)),
        "cell_count": draw_cell_count(jax.random.fold_in(jax.random.fold_in(keys[5], part), 71), part),
        "cell_target": draw_cell_target(jax.random.fold_in(jax.random.fold_in(keys[5], part), 71), part),
        "surface": draw_surface(jax.random.fold_in(jax.random.fold_in(keys[5], part), 71), part),
        "observers": draw_observers(jax.random.fold_in(jax.random.fold_in(keys[5], part), 71), part),
    }


def spectral_lookup_matrix(signal_readings):
    clock_moments = jnp.arange(signal_readings, dtype=jnp.int32)
    spectral_slot_number = jnp.arange(NF, dtype=jnp.int32) + signal_readings // 16
    modulo_angle_value = spectral_slot_number[:, None] * clock_moments[None, :] % signal_readings
    phases = 2.0 * math.pi / signal_readings * modulo_angle_value.astype(jnp.float32)
    hann_attenuation_curve = 0.5 - 0.5 * jnp.cos(2.0 * math.pi / signal_readings * clock_moments.astype(jnp.float32))
    scaled = 2.0 / signal_readings * hann_attenuation_curve[None, :]
    return jnp.concatenate([scaled * jnp.cos(phases), -scaled * jnp.sin(phases)], axis=0).astype(jnp.bfloat16)

def radiate(spectra, surface, listeners, amplitude):
    delta_x = listeners[0][:, None] - surface[0][None, :]
    delta_y = listeners[1][:, None] - surface[1][None, :]
    delta_z = listeners[2][:, None] - surface[2][None, :]
    radius = jnp.sqrt(delta_x * delta_x + delta_y * delta_y + delta_z * delta_z)
    inverse = 1.0 / radius
    normal_x = delta_x * inverse
    normal_y = delta_y * inverse
    normal_z = delta_z * inverse
    quadrature_factor = surface[3][None, :] * inverse * (amplitude / (4.0 * math.pi))
    blocks = spectra.reshape(2, NF, 4, spectra.shape[1])
    real_list = []
    imag_list = []
    for harmonic in range(NF):
        wavenumber = 0.5 + 0.25 * harmonic
        real_part = blocks[0, harmonic]
        imag_part = blocks[1, harmonic]
        load_real = real_part[1][None, :] * normal_x + real_part[2][None, :] * normal_y + real_part[3][None, :] * normal_z
        load_imag = imag_part[1][None, :] * normal_x + imag_part[2][None, :] * normal_y + imag_part[3][None, :] * normal_z
        source_real = -wavenumber * imag_part[0][None, :] + load_real * inverse - wavenumber * load_imag
        source_imag = wavenumber * real_part[0][None, :] + wavenumber * load_real + load_imag * inverse
        cosine = jnp.cos(wavenumber * radius)
        sinusoid = jnp.sin(wavenumber * radius)
        real_list.append(lax.optimization_barrier(jnp.sum(quadrature_factor * (source_real * cosine + source_imag * sinusoid), axis=1)))
        imag_list.append(lax.optimization_barrier(jnp.sum(quadrature_factor * (source_imag * cosine - source_real * sinusoid), axis=1)))
    real_out = jnp.stack(real_list, axis=1)
    imag_out = jnp.stack(imag_list, axis=1)
    return jnp.stack([real_out, imag_out], axis=1)

def reference(cell_series, cell_count, cell_target, surface, observers):
    twiddle = spectral_lookup_matrix(NT)
    flattened = cell_series.reshape(ROWS * 4, NT)
    per_cell = jnp.dot(flattened, twiddle.T, preferred_element_type=jnp.float32)
    per_cell = per_cell.reshape(ROWS, 4, 2 * NF).transpose(0, 2, 1).reshape(ROWS, 8 * NF)
    row_index = jnp.arange(ROWS, dtype=jnp.int32)
    device = row_index // R_DEV
    active = row_index % R_DEV < cell_count[device]
    owner_index = cell_target // P_DEV
    point_index = ((owner_index * N_SUB + device % N_SUB) * P_DEV + cell_target % P_DEV).astype(jnp.int32)
    per_cell = jnp.where(active[:, None], per_cell, jnp.zeros_like(per_cell))
    per_point = jax.ops.segment_sum(per_cell, point_index, num_segments=NPTS)
    spectra = per_point.T
    amplitude = 150.0 * math.sqrt(NT * P_DEV / (R_DEV * NPTS))
    listeners = observers.reshape(3, N_BLK, OBS_BLK).transpose(1, 0, 2)
    result = lax.map(lambda listener_block: radiate(spectra, surface, listener_block, amplitude), listeners)
    return result.reshape(NOBS, 2, NF)
```

```python
import math

import jax
import jax.numpy as jnp
from jax import lax
from jax.experimental import pallas as pl
from jax.experimental.pallas import tpu as pltpu
from jax.sharding import PartitionSpec as P

NF = 8
MESH = pl.DeviceIdType.MESH


def polynomials(terms):
    import numpy as np

    nodes = np.cos((np.arange(400) + 0.5) * np.pi / 400)
    squares = (nodes + 1.0) * 0.125
    u = np.sqrt(squares)
    out = []
    for values in (np.sin(2 * np.pi * u) / u, np.cos(2 * np.pi * u)):
        series = np.polynomial.chebyshev.chebfit(nodes, values, terms - 1)
        powers = np.polynomial.chebyshev.cheb2poly(series)
        total = np.zeros(1)
        for a in powers[::-1]:
            total = np.polynomial.polynomial.polyadd(
                np.polynomial.polynomial.polymul(total, [-1.0, 8.0]), [a]
            )
        out.append([float(np.float32(c)) for c in total[:terms]])
    return out


def spectral_lookup_matrix(signal_readings):
    clock_moments = jnp.arange(signal_readings, dtype=jnp.int32)
    spectral_slot_number = jnp.arange(NF, dtype=jnp.int32) + signal_readings // 16
    modulo_angle_value = spectral_slot_number[:, None] * clock_moments[None, :] % signal_readings
    phases = 2.0 * math.pi / signal_readings * modulo_angle_value.astype(jnp.float32)
    hann_attenuation_curve = 0.5 - 0.5 * jnp.cos(
        2.0 * math.pi / signal_readings * clock_moments.astype(jnp.float32)
    )
    scaled = 2.0 / signal_readings * hann_attenuation_curve[None, :]
    return jnp.concatenate([scaled * jnp.cos(phases), -scaled * jnp.sin(phases)], axis=0).astype(
        jnp.bfloat16
    )


def horner(coefficients, v):
    total = coefficients[-1] * v + coefficients[-2]
    for c in coefficients[-3::-1]:
        total = total * v + c
    return total


def make_kernel(n_blk, n_split, n_sub, rows, points, n_obs, amplitude):
    groups = n_blk * n_split
    devices = groups * n_sub
    obs_blk = n_obs // n_blk
    sin_c, cos_c = polynomials(7)
    half = 256 if n_obs % 256 == 0 else n_obs
    step_q = 16

    def each(count, body):
        lax.fori_loop(1, count, lambda i, c: (body(i), c)[1], 0, unroll=count <= 16)

    def kernel(
        pc_ref, count_ref, target_ref, surface_ref, surface_t_ref, obs_ref, out_ref,
        stage, recv, green, rows_scr, out_scr, press, recv2,
        send_sem, recv_sem, send_sem2, recv_sem2,
    ):
        blk = lax.axis_index("blk")
        split = lax.axis_index("split")
        sub = lax.axis_index("sub")
        group = blk * n_split + split
        me = group * n_sub + sub

        def device(index):
            g = index // n_sub
            return {"blk": g // n_split, "split": g % n_split, "sub": index % n_sub}

        barrier = pltpu.get_barrier_semaphore()

        def greet(i):
            pl.semaphore_signal(
                barrier, inc=1, device_id=device(lax.rem(me + i, devices)), device_id_type=MESH
            )

        each(devices, greet)

        pc = pc_ref[...]
        high = pc.astype(jnp.bfloat16)
        low = (pc - high.astype(jnp.float32)).astype(jnp.bfloat16)
        both = jnp.concatenate([high, low], axis=0)
        live = lax.broadcasted_iota(jnp.int32, (1, rows), 1) < count_ref[0]
        target = jnp.where(live, target_ref[...], -1)
        point = lax.broadcasted_iota(jnp.int32, (points, rows), 0)

        def partial_sums(g):
            chosen = (point == target - g * points).astype(jnp.float32).astype(jnp.bfloat16)
            sums = lax.dot_general(
                both, chosen, (((1,), (1,)), ((), ())), preferred_element_type=jnp.float32
            )
            return (sums[: 8 * NF] + sums[8 * NF :]).astype(jnp.bfloat16)

        def spectra_copy(i):
            g = lax.rem(group + i, groups)
            return pltpu.make_async_remote_copy(
                src_ref=stage.at[i],
                dst_ref=recv.at[i],
                send_sem=send_sem.at[i],
                recv_sem=recv_sem.at[i],
                device_id={"blk": g // n_split, "split": g % n_split, "sub": sub},
                device_id_type=MESH,
            )

        pl.semaphore_wait(barrier, devices - 1)

        def send_spectra(i):
            stage[i] = partial_sums(lax.rem(group + i, groups))
            spectra_copy(i).start()

        each(groups, send_spectra)
        stage[0] = partial_sums(group)

        def green_step(step, carry):
            start = pl.multiple_of(step * step_q, step_q)
            at = surface_t_ref[pl.ds(start, step_q), :]
            for h in range(n_obs // half):
                lanes = pl.ds(h * half, half)
                d_x = obs_ref[0:1, lanes] - at[:, 0:1]
                d_y = obs_ref[1:2, lanes] - at[:, 1:2]
                d_z = obs_ref[2:3, lanes] - at[:, 2:3]
                square = d_x * d_x + d_y * d_y + d_z * d_z
                inverse = lax.rsqrt(square)
                radius = square * inverse
                turns = radius * (0.25 / (2.0 * math.pi))
                turns = turns - jnp.round(turns)
                v = turns * turns
                cosine = horner(cos_c, v)
                sine = horner(sin_c, v) * turns
                twice = cosine + cosine
                scale = inverse * inverse
                old_r = cosine * scale
                old_i = -sine * scale
                new_r = twice * old_r - scale
                new_i = twice * old_i
                for f in range(NF):
                    k = 0.5 + 0.25 * f
                    base = f * 4 * points + start
                    parts = (
                        new_r * radius,
                        new_i * radius,
                        new_r * inverse - k * new_i,
                        new_i * inverse + k * new_r,
                    )
                    for p, value in enumerate(parts):
                        green[pl.ds(base + p * points, step_q), lanes] = value.astype(jnp.bfloat16)
                    old_r, new_r = new_r, twice * new_r - old_r
                    old_i, new_i = new_i, twice * new_i - old_i
            return carry

        lax.fori_loop(0, points // step_q, green_step, 0)

        each(groups, lambda i: spectra_copy(i).wait_recv())
        if groups <= 16:
            spectra = stage[0].astype(jnp.float32)
            for i in range(1, groups):
                spectra += recv[i].astype(jnp.float32)
        else:
            spectra = lax.fori_loop(
                1, groups, lambda i, s: s + recv[i].astype(jnp.float32), stage[0].astype(jnp.float32)
            )
        surface = surface_ref[...]
        spectra = spectra * (surface[3:4] * (amplitude / (4.0 * math.pi)))
        wave = 0.5 + 0.25 * lax.broadcasted_iota(jnp.int32, (NF, points), 0).astype(jnp.float32)
        part = [
            (spectra[16 * c : 16 * c + NF], spectra[16 * c + NF : 16 * c + 2 * NF]) for c in range(4)
        ]
        mono_r = -wave * part[0][1]
        mono_i = wave * part[0][0]
        along_r = sum(surface[c : c + 1] * part[c + 1][0] for c in range(3))
        along_i = sum(surface[c : c + 1] * part[c + 1][1] for c in range(3))
        zero = jnp.zeros_like(wave)
        lines = [(mono_r, -mono_i, -along_r, along_i), (mono_i, mono_r, -along_i, -along_r)]
        for c in range(1, 4):
            r, i = part[c]
            lines.append((zero, zero, r, -i))
            lines.append((zero, zero, i, r))
        for t, line in enumerate(lines):
            for p, value in enumerate(line):
                for q in range(points // 128):
                    rows_scr[p * (points // 128) + q, t * NF : (t + 1) * NF, :] = value[
                        :, q * 128 : (q + 1) * 128
                    ]
        for f in range(NF):
            left = jnp.concatenate(
                [
                    rows_scr[p, pl.ds(f, 8, stride=NF), :]
                    for p in range(4 * points // 128)
                ],
                axis=1,
            )
            left_high = left.astype(jnp.bfloat16).astype(jnp.float32)
            left = jnp.concatenate([left_high, left - left_high], axis=0).astype(jnp.bfloat16)
            result = jnp.dot(
                left,
                green[f * 4 * points : (f + 1) * 4 * points, :],
                preferred_element_type=jnp.float32,
            )
            result = result[:8] + result[8:]
            for q in range(n_obs // 128):
                out_scr[q, f * 8 : (f + 1) * 8, :] = result[:, q * 128 : (q + 1) * 128]
        for b in range(n_blk):
            for lane in range(b * obs_blk, (b + 1) * obs_blk, 128):
                lanes = slice(lane, lane + 128)
                terms = [out_scr[lane // 128, pl.ds(t, NF, stride=8), :] for t in range(8)]
                x, y, z = (obs_ref[c : c + 1, lanes] for c in range(3))
                inner = slice(lane - b * obs_blk, lane - b * obs_blk + 128)
                press[b, 0:NF, inner] = terms[0] + x * terms[2] + y * terms[4] + z * terms[6]
                press[b, NF : 2 * NF, inner] = terms[1] + x * terms[3] + y * terms[5] + z * terms[7]

        def pressure_copy(i):
            to = device(lax.rem(me + i, devices))
            return pltpu.make_async_remote_copy(
                src_ref=press.at[to["blk"]],
                dst_ref=recv2.at[i],
                send_sem=send_sem2.at[i],
                recv_sem=recv_sem2.at[i],
                device_id=to,
                device_id_type=MESH,
            )

        each(devices, lambda i: pressure_copy(i).start())
        each(groups, lambda i: spectra_copy(i).wait_send())
        each(devices, lambda i: pressure_copy(i).wait_recv())
        if devices <= 16:
            total = press[blk]
            for i in range(1, devices):
                total += recv2[i]
        else:
            total = lax.fori_loop(1, devices, lambda i, s: s + recv2[i], press[blk])
        out_ref[...] = total
        each(devices, lambda i: pressure_copy(i).wait_send())

    scratch = [
        pltpu.VMEM((groups, 8 * NF, points), jnp.bfloat16),
        pltpu.VMEM((groups, 8 * NF, points), jnp.bfloat16),
        pltpu.VMEM((NF * 4 * points, n_obs), jnp.bfloat16),
        pltpu.VMEM((4 * points // 128, 8 * NF, 128), jnp.float32),
        pltpu.VMEM((n_obs // 128, 8 * NF, 128), jnp.float32),
        pltpu.VMEM((n_blk, 2 * NF, obs_blk), jnp.float32),
        pltpu.VMEM((devices, 2 * NF, obs_blk), jnp.float32),
        pltpu.SemaphoreType.DMA((groups,)),
        pltpu.SemaphoreType.DMA((groups,)),
        pltpu.SemaphoreType.DMA((devices,)),
        pltpu.SemaphoreType.DMA((devices,)),
    ]
    vmem = pl.BlockSpec(memory_space=pltpu.VMEM)
    return pl.pallas_call(
        kernel,
        out_shape=jax.ShapeDtypeStruct((2 * NF, obs_blk), jnp.float32),
        in_specs=[vmem, pl.BlockSpec(memory_space=pltpu.SMEM), vmem, vmem, vmem, vmem],
        out_specs=vmem,
        scratch_shapes=scratch,
        compiler_params=pltpu.CompilerParams(
            collective_id=0, has_side_effects=True, vmem_limit_bytes=56 * 2**20
        ),
    )


def local(cell_series, cell_count, cell_target, surface, observers):
    rows_dev, _, signal_readings = cell_series.shape
    points_dev = surface.shape[1]
    n_blk, n_split, n_sub = (lax.axis_size(a) for a in ("blk", "split", "sub"))
    devices = n_blk * n_split * n_sub
    amplitude = 150.0 * math.sqrt(
        signal_readings * points_dev / (rows_dev * (points_dev * devices))
    )
    twiddle = spectral_lookup_matrix(signal_readings)
    per_cell = jnp.einsum("jt,rct->cjr", twiddle, cell_series, preferred_element_type=jnp.float32)
    kernel = make_kernel(n_blk, n_split, n_sub, rows_dev, points_dev, observers.shape[1], amplitude)
    pressure = kernel(
        per_cell.reshape(8 * NF, rows_dev),
        cell_count,
        cell_target.reshape(1, rows_dev),
        surface,
        surface.T,
        observers,
    )
    return pressure.T.reshape(observers.shape[1] // n_blk, 2, NF)


def solution(mesh):
    return jax.shard_map(
        local,
        mesh=mesh,
        in_specs=(
            P(("case", "blk", "split", "sub"), None, None),
            P(("case", "blk", "split", "sub")),
            P(("case", "blk", "split", "sub")),
            P(None, ("case", "blk", "split", "sub")),
            P(None, "case"),
        ),
        out_specs=P(("case", "blk"), None, None),
        check_vma=False,
    )
```

```python
import math

import jax
import jax.numpy as jnp
from jax import lax
from jax.experimental import pallas as pl
from jax.experimental.pallas import tpu as pltpu
from jax.sharding import PartitionSpec as P

NF = 8
MESH = pl.DeviceIdType.MESH


def polynomials(terms):
    import numpy as np

    nodes = np.cos((np.arange(400) + 0.5) * np.pi / 400)
    squares = (nodes + 1.0) * 0.125
    u = np.sqrt(squares)
    out = []
    for values in (np.sin(2 * np.pi * u) / u, np.cos(2 * np.pi * u)):
        series = np.polynomial.chebyshev.chebfit(nodes, values, terms - 1)
        powers = np.polynomial.chebyshev.cheb2poly(series)
        total = np.zeros(1)
        for a in powers[::-1]:
            total = np.polynomial.polynomial.polyadd(
                np.polynomial.polynomial.polymul(total, [-1.0, 8.0]), [a]
            )
        out.append([float(np.float32(c)) for c in total[:terms]])
    return out


def spectral_lookup_matrix(signal_readings):
    clock_moments = jnp.arange(signal_readings, dtype=jnp.int32)
    spectral_slot_number = jnp.arange(NF, dtype=jnp.int32) + signal_readings // 16
    modulo_angle_value = spectral_slot_number[:, None] * clock_moments[None, :] % signal_readings
    phases = 2.0 * math.pi / signal_readings * modulo_angle_value.astype(jnp.float32)
    hann_attenuation_curve = 0.5 - 0.5 * jnp.cos(
        2.0 * math.pi / signal_readings * clock_moments.astype(jnp.float32)
    )
    scaled = 2.0 / signal_readings * hann_attenuation_curve[None, :]
    return jnp.concatenate([scaled * jnp.cos(phases), -scaled * jnp.sin(phases)], axis=0).astype(
        jnp.bfloat16
    )


def horner(coefficients, v):
    total = coefficients[-1] * v + coefficients[-2]
    for c in coefficients[-3::-1]:
        total = total * v + c
    return total


def make_kernel(n_blk, n_split, n_sub, rows, points, n_obs, amplitude):
    groups = n_blk * n_split
    places = n_split * n_sub
    obs_blk = n_obs // n_blk
    sin_c, cos_c = polynomials(7)
    half = 256 if n_obs % 256 == 0 else n_obs
    step_q = 16

    def each(count, body):
        lax.fori_loop(1, count, lambda i, c: (body(i), c)[1], 0, unroll=count <= 16)

    def kernel(
        pc_ref, count_ref, target_ref, surface_ref, obs_ref, out_ref,
        stage, recv, green, rows_scr, out_scr, press, recv2, recv3, surface_t_ref,
        send_sem, recv_sem, send_sem2, recv_sem2, send_sem3, recv_sem3,
    ):
        blk = lax.axis_index("blk")
        split = lax.axis_index("split")
        sub = lax.axis_index("sub")
        group = blk * n_split + split
        place = split * n_sub + sub

        def group_device(i):
            g = lax.rem(group + i, groups)
            return {"blk": g // n_split, "split": lax.rem(g, n_split), "sub": sub}

        def block_device(i):
            return {"blk": lax.rem(blk + i, n_blk), "split": split, "sub": sub}

        def place_device(i):
            p = lax.rem(place + i, places)
            return {"blk": blk, "split": p // n_sub, "sub": lax.rem(p, n_sub)}

        barrier = pltpu.get_barrier_semaphore()

        def greet(to):
            pl.semaphore_signal(barrier, inc=1, device_id=to, device_id_type=MESH)

        each(groups, lambda i: greet(group_device(i)))
        for other in range(1, n_sub):
            for at_split in range(n_split):
                greet({"blk": blk, "split": at_split, "sub": lax.rem(sub + other, n_sub)})

        pc = pc_ref[...]
        high = pc.astype(jnp.bfloat16)
        low = (pc - high.astype(jnp.float32)).astype(jnp.bfloat16)
        both = jnp.concatenate([high, low], axis=0)
        live = lax.broadcasted_iota(jnp.int32, (1, rows), 1) < count_ref[0]
        target = jnp.where(live, target_ref[...], -1)
        point = lax.broadcasted_iota(jnp.int32, (points, rows), 0)

        def partial_sums(g):
            chosen = (point == target - g * points).astype(jnp.float32).astype(jnp.bfloat16)
            sums = lax.dot_general(
                both, chosen, (((1,), (1,)), ((), ())), preferred_element_type=jnp.float32
            )
            return (sums[: 8 * NF] + sums[8 * NF :]).astype(jnp.bfloat16)

        def spectra_copy(i):
            return pltpu.make_async_remote_copy(
                src_ref=stage.at[i],
                dst_ref=recv.at[i],
                send_sem=send_sem.at[i],
                recv_sem=recv_sem.at[i],
                device_id=group_device(i),
                device_id_type=MESH,
            )

        pl.semaphore_wait(barrier, groups - 1 + n_split * (n_sub - 1))

        def send_spectra(i):
            stage[i] = partial_sums(lax.rem(group + i, groups))
            spectra_copy(i).start()

        each(groups, send_spectra)
        stage[0] = partial_sums(group)

        surface = surface_ref[...]
        surface_t_ref[...] = jnp.concatenate([surface, surface], axis=0).T

        def green_step(step, carry):
            start = pl.multiple_of(step * step_q, step_q)
            at = surface_t_ref[pl.ds(start, step_q), :]
            for h in range(n_obs // half):
                lanes = pl.ds(h * half, half)
                d_x = obs_ref[0:1, lanes] - at[:, 0:1]
                d_y = obs_ref[1:2, lanes] - at[:, 1:2]
                d_z = obs_ref[2:3, lanes] - at[:, 2:3]
                square = d_x * d_x + d_y * d_y + d_z * d_z
                inverse = lax.rsqrt(square)
                radius = square * inverse
                turns = radius * (0.25 / (2.0 * math.pi))
                turns = turns - jnp.round(turns)
                v = turns * turns
                cosine = horner(cos_c, v)
                sine = horner(sin_c, v) * turns
                twice = cosine + cosine
                scale = inverse * inverse
                old_r = cosine * scale
                old_i = -sine * scale
                new_r = twice * old_r - scale
                new_i = twice * old_i
                for f in range(NF):
                    k = 0.5 + 0.25 * f
                    base = f * 4 * points + start
                    parts = (
                        new_r * radius,
                        new_i * radius,
                        new_r * inverse - k * new_i,
                        new_i * inverse + k * new_r,
                    )
                    for p, value in enumerate(parts):
                        green[pl.ds(base + p * points, step_q), lanes] = value.astype(jnp.bfloat16)
                    old_r, new_r = new_r, twice * new_r - old_r
                    old_i, new_i = new_i, twice * new_i - old_i
            return carry

        lax.fori_loop(0, points // step_q, green_step, 0)

        each(groups, lambda i: spectra_copy(i).wait_recv())
        if groups <= 16:
            spectra = stage[0].astype(jnp.float32)
            for i in range(1, groups):
                spectra += recv[i].astype(jnp.float32)
        else:
            spectra = lax.fori_loop(
                1, groups, lambda i, s: s + recv[i].astype(jnp.float32), stage[0].astype(jnp.float32)
            )
        spectra = spectra * (surface[3:4] * (amplitude / (4.0 * math.pi)))
        wave = 0.5 + 0.25 * lax.broadcasted_iota(jnp.int32, (NF, points), 0).astype(jnp.float32)
        part = [
            (spectra[16 * c : 16 * c + NF], spectra[16 * c + NF : 16 * c + 2 * NF]) for c in range(4)
        ]
        mono_r = -wave * part[0][1]
        mono_i = wave * part[0][0]
        along_r = sum(surface[c : c + 1] * part[c + 1][0] for c in range(3))
        along_i = sum(surface[c : c + 1] * part[c + 1][1] for c in range(3))
        zero = jnp.zeros_like(wave)
        lines = [(mono_r, -mono_i, -along_r, along_i), (mono_i, mono_r, -along_i, -along_r)]
        for c in range(1, 4):
            r, i = part[c]
            lines.append((zero, zero, r, -i))
            lines.append((zero, zero, i, r))
        for t, line in enumerate(lines):
            for p, value in enumerate(line):
                for q in range(points // 128):
                    rows_scr[p * (points // 128) + q, t * NF : (t + 1) * NF, :] = value[
                        :, q * 128 : (q + 1) * 128
                    ]
        for f in range(NF):
            left = jnp.concatenate(
                [
                    rows_scr[p, pl.ds(f, 8, stride=NF), :]
                    for p in range(4 * points // 128)
                ],
                axis=1,
            )
            left_high = left.astype(jnp.bfloat16).astype(jnp.float32)
            left = jnp.concatenate([left_high, left - left_high], axis=0).astype(jnp.bfloat16)
            result = jnp.dot(
                left,
                green[f * 4 * points : (f + 1) * 4 * points, :],
                preferred_element_type=jnp.float32,
            )
            result = result[:8] + result[8:]
            for q in range(n_obs // 128):
                out_scr[q, f * 8 : (f + 1) * 8, :] = result[:, q * 128 : (q + 1) * 128]
        for b in range(n_blk):
            for lane in range(b * obs_blk, (b + 1) * obs_blk, 128):
                lanes = slice(lane, lane + 128)
                terms = [out_scr[lane // 128, pl.ds(t, NF, stride=8), :] for t in range(8)]
                x, y, z = (obs_ref[c : c + 1, lanes] for c in range(3))
                inner = slice(lane - b * obs_blk, lane - b * obs_blk + 128)
                press[b, 0:NF, inner] = terms[0] + x * terms[2] + y * terms[4] + z * terms[6]
                press[b, NF : 2 * NF, inner] = terms[1] + x * terms[3] + y * terms[5] + z * terms[7]

        def block_copy(i):
            return pltpu.make_async_remote_copy(
                src_ref=press.at[lax.rem(blk + i, n_blk)],
                dst_ref=recv2.at[i],
                send_sem=send_sem2.at[i],
                recv_sem=recv_sem2.at[i],
                device_id=block_device(i),
                device_id_type=MESH,
            )

        def place_copy(i):
            return pltpu.make_async_remote_copy(
                src_ref=recv3.at[0],
                dst_ref=recv3.at[i],
                send_sem=send_sem3.at[i],
                recv_sem=recv_sem3.at[i],
                device_id=place_device(i),
                device_id_type=MESH,
            )

        def summed(ref, count, first):
            if count > 16:
                return lax.fori_loop(1, count, lambda i, s: s + ref[i], first)
            for i in range(1, count):
                first += ref[i]
            return first

        each(n_blk, lambda i: block_copy(i).start())
        each(groups, lambda i: spectra_copy(i).wait_send())
        each(n_blk, lambda i: block_copy(i).wait_recv())
        total = summed(recv2, n_blk, press[blk])
        recv3[0] = total
        each(places, lambda i: place_copy(i).start())
        each(n_blk, lambda i: block_copy(i).wait_send())
        each(places, lambda i: place_copy(i).wait_recv())
        out_ref[...] = summed(recv3, places, total)
        each(places, lambda i: place_copy(i).wait_send())

    scratch = [
        pltpu.VMEM((groups, 8 * NF, points), jnp.bfloat16),
        pltpu.VMEM((groups, 8 * NF, points), jnp.bfloat16),
        pltpu.VMEM((NF * 4 * points, n_obs), jnp.bfloat16),
        pltpu.VMEM((4 * points // 128, 8 * NF, 128), jnp.float32),
        pltpu.VMEM((n_obs // 128, 8 * NF, 128), jnp.float32),
        pltpu.VMEM((n_blk, 2 * NF, obs_blk), jnp.float32),
        pltpu.VMEM((n_blk, 2 * NF, obs_blk), jnp.float32),
        pltpu.VMEM((places, 2 * NF, obs_blk), jnp.float32),
        pltpu.VMEM((points, 8), jnp.float32),
        pltpu.SemaphoreType.DMA((groups,)),
        pltpu.SemaphoreType.DMA((groups,)),
        pltpu.SemaphoreType.DMA((n_blk,)),
        pltpu.SemaphoreType.DMA((n_blk,)),
        pltpu.SemaphoreType.DMA((places,)),
        pltpu.SemaphoreType.DMA((places,)),
    ]
    vmem = pl.BlockSpec(memory_space=pltpu.VMEM)
    return pl.pallas_call(
        kernel,
        out_shape=jax.ShapeDtypeStruct((2 * NF, obs_blk), jnp.float32),
        in_specs=[vmem, pl.BlockSpec(memory_space=pltpu.SMEM), vmem, vmem, vmem],
        out_specs=vmem,
        scratch_shapes=scratch,
        compiler_params=pltpu.CompilerParams(
            collective_id=0, has_side_effects=True, vmem_limit_bytes=56 * 2**20
        ),
    )


def local(cell_series, cell_count, cell_target, surface, observers):
    rows_dev, _, signal_readings = cell_series.shape
    points_dev = surface.shape[1]
    n_blk, n_split, n_sub = (lax.axis_size(a) for a in ("blk", "split", "sub"))
    devices = n_blk * n_split * n_sub
    amplitude = 150.0 * math.sqrt(
        signal_readings * points_dev / (rows_dev * (points_dev * devices))
    )
    twiddle = spectral_lookup_matrix(signal_readings)
    per_cell = jnp.einsum("jt,rct->cjr", twiddle, cell_series, preferred_element_type=jnp.float32)
    kernel = make_kernel(n_blk, n_split, n_sub, rows_dev, points_dev, observers.shape[1], amplitude)
    pressure = kernel(
        per_cell.reshape(8 * NF, rows_dev),
        cell_count,
        cell_target.reshape(1, rows_dev),
        surface,
        observers,
    )
    return pressure.T.reshape(observers.shape[1] // n_blk, 2, NF)


def solution(mesh):
    return jax.shard_map(
        local,
        mesh=mesh,
        in_specs=(
            P(("case", "blk", "split", "sub"), None, None),
            P(("case", "blk", "split", "sub")),
            P(("case", "blk", "split", "sub")),
            P(None, ("case", "blk", "split", "sub")),
            P(None, "case"),
        ),
        out_specs=P(("case", "blk"), None, None),
        check_vma=False,
    )
```

```python
import math

import jax
import jax.numpy as jnp
from jax import lax
from jax.experimental import pallas as pl
from jax.experimental.pallas import tpu as pltpu
from jax.sharding import PartitionSpec as P

NF = 8
MESH = pl.DeviceIdType.MESH


def polynomials(terms):
    import numpy as np

    nodes = np.cos((np.arange(400) + 0.5) * np.pi / 400)
    squares = (nodes + 1.0) * 0.125
    u = np.sqrt(squares)
    out = []
    for values in (np.sin(2 * np.pi * u) / u, np.cos(2 * np.pi * u)):
        series = np.polynomial.chebyshev.chebfit(nodes, values, terms - 1)
        powers = np.polynomial.chebyshev.cheb2poly(series)
        total = np.zeros(1)
        for a in powers[::-1]:
            total = np.polynomial.polynomial.polyadd(
                np.polynomial.polynomial.polymul(total, [-1.0, 8.0]), [a]
            )
        out.append([float(np.float32(c)) for c in total[:terms]])
    return out


def spectral_lookup_matrix(signal_readings):
    clock_moments = jnp.arange(signal_readings, dtype=jnp.int32)
    spectral_slot_number = jnp.arange(NF, dtype=jnp.int32) + signal_readings // 16
    modulo_angle_value = spectral_slot_number[:, None] * clock_moments[None, :] % signal_readings
    phases = 2.0 * math.pi / signal_readings * modulo_angle_value.astype(jnp.float32)
    hann_attenuation_curve = 0.5 - 0.5 * jnp.cos(
        2.0 * math.pi / signal_readings * clock_moments.astype(jnp.float32)
    )
    scaled = 2.0 / signal_readings * hann_attenuation_curve[None, :]
    return jnp.concatenate([scaled * jnp.cos(phases), -scaled * jnp.sin(phases)], axis=0).astype(
        jnp.bfloat16
    )


def horner(coefficients, v):
    total = coefficients[-1] * v + coefficients[-2]
    for c in coefficients[-3::-1]:
        total = total * v + c
    return total


def make_kernel(n_blk, n_split, n_sub, rows, samples, points, n_obs, amplitude):
    chunk = 128
    groups = n_blk * n_split
    devices = groups * n_sub
    obs_blk = n_obs // n_blk
    sin_c, cos_c = polynomials(7)
    half = 256 if n_obs % 256 == 0 else n_obs
    step_q = 16

    def each(count, body, first=1):
        lax.fori_loop(first, count, lambda i, c: (body(i), c)[1], 0)

    def kernel(
        series_ref, twiddle_ref, count_ref, target_ref, surface_ref, obs_ref, out_ref,
        series, per_cell, stage, recv, green, rows_scr, out_scr, press, recv2, surface_t_ref,
        load_sem, send_sem, recv_sem, send_sem2, recv_sem2,
    ):
        blk = lax.axis_index("blk")
        split = lax.axis_index("split")
        sub = lax.axis_index("sub")
        group = blk * n_split + split
        me = group * n_sub + sub

        def group_device(i):
            g = lax.rem(group + i, groups)
            return {"blk": g // n_split, "split": lax.rem(g, n_split), "sub": sub}

        def any_device(i):
            to = lax.rem(me + i, devices)
            g = to // n_sub
            return {"blk": g // n_split, "split": lax.rem(g, n_split), "sub": lax.rem(to, n_sub)}

        def total(ref, count):
            if count <= 16:
                return sum(ref[i].astype(jnp.float32) for i in range(count))
            zero = jnp.zeros(ref.shape[1:], jnp.float32)
            return lax.fori_loop(0, count, lambda i, s: s + ref[i].astype(jnp.float32), zero)

        def load(i):
            cells = pl.ds(i * chunk, chunk)
            return pltpu.make_async_copy(series_ref.at[cells], series.at[cells], load_sem.at[i])

        each(rows // chunk, lambda i: load(i).start(), 0)

        barrier = pltpu.get_barrier_semaphore()

        def greet(i):
            pl.semaphore_signal(barrier, inc=1, device_id=any_device(i), device_id_type=MESH)

        each(devices, greet)

        twiddle = twiddle_ref[...]

        def transform(i):
            load(i).wait()
            records = pl.ds(pl.multiple_of(4 * i * chunk, 4 * chunk), 4 * chunk)
            per_cell[records, :] = lax.dot_general(
                series[pl.ds(i * chunk, chunk)].reshape(4 * chunk, samples),
                twiddle,
                (((1,), (1,)), ((), ())),
                preferred_element_type=jnp.float32,
            )

        each(rows // chunk, transform, 0)
        lane = lax.broadcasted_iota(jnp.int32, (rows, 128), 1)
        component = lane // (2 * NF) % 4
        spectrum = per_cell[pl.ds(0, rows, stride=4), :]
        for c in range(1, 4):
            spectrum = jnp.where(component == c, per_cell[pl.ds(c, rows, stride=4), :], spectrum)
        high = spectrum.astype(jnp.bfloat16).astype(jnp.float32)
        both = jnp.where(lane < 8 * NF, high, spectrum - high).T.astype(jnp.bfloat16)
        live = lax.broadcasted_iota(jnp.int32, (1, rows), 1) < count_ref[0]
        target = jnp.where(live, target_ref[...], -1)
        point = lax.broadcasted_iota(jnp.int32, (points, rows), 0)

        def partial_sums(g):
            chosen = (point == target - g * points).astype(jnp.float32).astype(jnp.bfloat16)
            sums = lax.dot_general(
                both, chosen, (((1,), (1,)), ((), ())), preferred_element_type=jnp.float32
            )
            return (sums[: 8 * NF] + sums[8 * NF :]).astype(jnp.bfloat16)

        def spectra_copy(i):
            return pltpu.make_async_remote_copy(
                src_ref=stage.at[i],
                dst_ref=recv.at[i],
                send_sem=send_sem.at[i],
                recv_sem=recv_sem.at[i],
                device_id=group_device(i),
                device_id_type=MESH,
            )

        pl.semaphore_wait(barrier, devices - 1)

        def send_spectra(i):
            stage[i] = partial_sums(lax.rem(group + i, groups))
            spectra_copy(i).start()

        each(groups, send_spectra)
        recv[0] = partial_sums(group)

        surface = surface_ref[...]
        surface_t_ref[...] = jnp.concatenate([surface, surface], axis=0).T

        def green_step(step, carry):
            start = pl.multiple_of(step * step_q, step_q)
            at = surface_t_ref[pl.ds(start, step_q), :]
            for h in range(n_obs // half):
                lanes = pl.ds(h * half, half)
                d_x = obs_ref[0:1, lanes] - at[:, 0:1]
                d_y = obs_ref[1:2, lanes] - at[:, 1:2]
                d_z = obs_ref[2:3, lanes] - at[:, 2:3]
                square = d_x * d_x + d_y * d_y + d_z * d_z
                inverse = lax.rsqrt(square)
                radius = square * inverse
                turns = radius * (0.25 / (2.0 * math.pi))
                turns = turns - jnp.round(turns)
                v = turns * turns
                cosine = horner(cos_c, v)
                sine = horner(sin_c, v) * turns
                twice = cosine + cosine
                scale = inverse * inverse
                old_r = cosine * scale
                old_i = -sine * scale
                new_r = twice * old_r - scale
                new_i = twice * old_i
                for f in range(NF):
                    k = 0.5 + 0.25 * f
                    base = f * 4 * points + start
                    parts = (
                        new_r * radius,
                        new_i * radius,
                        new_r * inverse - k * new_i,
                        new_i * inverse + k * new_r,
                    )
                    for p, value in enumerate(parts):
                        green[pl.ds(base + p * points, step_q), lanes] = value.astype(jnp.bfloat16)
                    old_r, new_r = new_r, twice * new_r - old_r
                    old_i, new_i = new_i, twice * new_i - old_i
            return carry

        lax.fori_loop(0, points // step_q, green_step, 0)

        each(groups, lambda i: spectra_copy(i).wait_recv())
        spectra = total(recv, groups)
        spectra = spectra * (surface[3:4] * (amplitude / (4.0 * math.pi)))
        wave = 0.5 + 0.25 * lax.broadcasted_iota(jnp.int32, (NF, points), 0).astype(jnp.float32)
        part = [
            (spectra[16 * c : 16 * c + NF], spectra[16 * c + NF : 16 * c + 2 * NF]) for c in range(4)
        ]
        mono_r = -wave * part[0][1]
        mono_i = wave * part[0][0]
        along_r = sum(surface[c : c + 1] * part[c + 1][0] for c in range(3))
        along_i = sum(surface[c : c + 1] * part[c + 1][1] for c in range(3))
        zero = jnp.zeros_like(wave)
        lines = [(mono_r, -mono_i, -along_r, along_i), (mono_i, mono_r, -along_i, -along_r)]
        for c in range(1, 4):
            r, i = part[c]
            lines.append((zero, zero, r, -i))
            lines.append((zero, zero, i, r))
        for t, line in enumerate(lines):
            for p, value in enumerate(line):
                for q in range(points // 128):
                    rows_scr[p * (points // 128) + q, t * NF : (t + 1) * NF, :] = value[
                        :, q * 128 : (q + 1) * 128
                    ]

        def radiate(f):
            left = jnp.concatenate(
                [rows_scr[p, pl.ds(f, 8, stride=NF), :] for p in range(4 * points // 128)], axis=1
            )
            left_high = left.astype(jnp.bfloat16).astype(jnp.float32)
            left = jnp.concatenate([left_high, left - left_high], axis=0).astype(jnp.bfloat16)
            result = jnp.dot(
                left,
                green[pl.ds(pl.multiple_of(f * 4 * points, 4 * points), 4 * points), :],
                preferred_element_type=jnp.float32,
            )
            result = result[:8] + result[8:]
            for q in range(n_obs // 128):
                out_scr[q, pl.ds(pl.multiple_of(f * 8, 8), 8), :] = result[:, q * 128 : (q + 1) * 128]

        each(NF, radiate, 0)
        for b in range(n_blk):
            for lane in range(b * obs_blk, (b + 1) * obs_blk, 128):
                lanes = slice(lane, lane + 128)
                terms = [out_scr[lane // 128, pl.ds(t, NF, stride=8), :] for t in range(8)]
                x, y, z = (obs_ref[c : c + 1, lanes] for c in range(3))
                inner = slice(lane - b * obs_blk, lane - b * obs_blk + 128)
                press[b, 0:NF, inner] = terms[0] + x * terms[2] + y * terms[4] + z * terms[6]
                press[b, NF : 2 * NF, inner] = terms[1] + x * terms[3] + y * terms[5] + z * terms[7]

        def pressure_copy(i):
            to = any_device(i)
            return pltpu.make_async_remote_copy(
                src_ref=press.at[to["blk"]],
                dst_ref=recv2.at[i],
                send_sem=send_sem2.at[i],
                recv_sem=recv_sem2.at[i],
                device_id=to,
                device_id_type=MESH,
            )

        each(devices, lambda i: pressure_copy(i).start())
        each(groups, lambda i: spectra_copy(i).wait_send())
        each(devices, lambda i: pressure_copy(i).wait_recv())
        recv2[0] = press[blk]
        out_ref[...] = total(recv2, devices)
        each(devices, lambda i: pressure_copy(i).wait_send())

    scratch = [
        pltpu.VMEM((rows, 4, samples), jnp.bfloat16),
        pltpu.VMEM((4 * rows, 128), jnp.float32),
        pltpu.VMEM((groups, 8 * NF, points), jnp.bfloat16),
        pltpu.VMEM((groups, 8 * NF, points), jnp.bfloat16),
        pltpu.VMEM((NF * 4 * points, n_obs), jnp.bfloat16),
        pltpu.VMEM((4 * points // 128, 8 * NF, 128), jnp.float32),
        pltpu.VMEM((n_obs // 128, 8 * NF, 128), jnp.float32),
        pltpu.VMEM((n_blk, 2 * NF, obs_blk), jnp.float32),
        pltpu.VMEM((devices, 2 * NF, obs_blk), jnp.float32),
        pltpu.VMEM((points, 8), jnp.float32),
        pltpu.SemaphoreType.DMA((rows // chunk,)),
        pltpu.SemaphoreType.DMA((groups,)),
        pltpu.SemaphoreType.DMA((groups,)),
        pltpu.SemaphoreType.DMA((devices,)),
        pltpu.SemaphoreType.DMA((devices,)),
    ]
    vmem = pl.BlockSpec(memory_space=pltpu.VMEM)
    return pl.pallas_call(
        kernel,
        out_shape=jax.ShapeDtypeStruct((2 * NF, obs_blk), jnp.float32),
        in_specs=[pl.BlockSpec(memory_space=pl.ANY), vmem, pl.BlockSpec(memory_space=pltpu.SMEM), vmem, vmem, vmem],
        out_specs=vmem,
        scratch_shapes=scratch,
        compiler_params=pltpu.CompilerParams(
            collective_id=0, has_side_effects=True, vmem_limit_bytes=56 * 2**20
        ),
    )


def local(cell_series, cell_count, cell_target, surface, observers):
    rows_dev, _, signal_readings = cell_series.shape
    points_dev = surface.shape[1]
    n_blk, n_split, n_sub = (lax.axis_size(a) for a in ("blk", "split", "sub"))
    devices = n_blk * n_split * n_sub
    amplitude = 150.0 * math.sqrt(
        signal_readings * points_dev / (rows_dev * (points_dev * devices))
    )
    twiddle = spectral_lookup_matrix(signal_readings)
    kernel = make_kernel(n_blk, n_split, n_sub, rows_dev, signal_readings, points_dev, observers.shape[1], amplitude)
    pressure = kernel(
        cell_series,
        jnp.concatenate([twiddle] * 8, axis=0),
        cell_count,
        cell_target.reshape(1, rows_dev),
        surface,
        observers,
    )
    return pressure.T.reshape(observers.shape[1] // n_blk, 2, NF)


def solution(mesh):
    return jax.shard_map(
        local,
        mesh=mesh,
        in_specs=(
            P(("case", "blk", "split", "sub"), None, None),
            P(("case", "blk", "split", "sub")),
            P(("case", "blk", "split", "sub")),
            P(None, ("case", "blk", "split", "sub")),
            P(None, "case"),
        ),
        out_specs=P(("case", "blk"), None, None),
        check_vma=False,
    )
```

```python
import math

import jax
import jax.numpy as jnp
import ml_dtypes
import numpy as np
from jax import lax
from jax.experimental import pallas as pl
from jax.experimental.pallas import tpu as pltpu
from jax.sharding import PartitionSpec as P

NF = 8
MESH = pl.DeviceIdType.MESH


def polynomials(terms):
    nodes = np.cos((np.arange(400) + 0.5) * np.pi / 400)
    squares = (nodes + 1.0) * 0.125
    u = np.sqrt(squares)
    out = []
    for values in (np.sin(2 * np.pi * u) / u, np.cos(2 * np.pi * u)):
        series = np.polynomial.chebyshev.chebfit(nodes, values, terms - 1)
        powers = np.polynomial.chebyshev.cheb2poly(series)
        total = np.zeros(1)
        for a in powers[::-1]:
            total = np.polynomial.polynomial.polyadd(
                np.polynomial.polynomial.polymul(total, [-1.0, 8.0]), [a]
            )
        out.append([float(np.float32(c)) for c in total[:terms]])
    return out


def spectral_lookup_matrix(signal_readings):
    moments = np.arange(signal_readings, dtype=np.int64)
    slots = np.arange(NF, dtype=np.int64) + signal_readings // 16
    modulo = slots[:, None] * moments[None, :] % signal_readings
    step = np.float32(2.0 * math.pi / signal_readings)
    phases = step * modulo.astype(np.float32)
    hann = np.float32(0.5) - np.float32(0.5) * np.cos(step * moments.astype(np.float32))
    scaled = np.float32(2.0 / signal_readings) * hann[None, :]
    table = np.concatenate([scaled * np.cos(phases), -scaled * np.sin(phases)], axis=0)
    return jnp.asarray(table.astype(ml_dtypes.bfloat16))


def horner(coefficients, v):
    total = coefficients[-1] * v + coefficients[-2]
    for c in coefficients[-3::-1]:
        total = total * v + c
    return total


def make_kernel(n_blk, n_split, n_sub, rows, samples, points, n_obs, amplitude):
    chunk = 128
    groups = n_blk * n_split
    devices = groups * n_sub
    obs_blk = n_obs // n_blk
    sin_c, cos_c = polynomials(7)
    half = 256 if n_obs % 256 == 0 else n_obs
    step_q = 16

    def each(count, body, first=1):
        lax.fori_loop(first, count, lambda i, c: (body(i), c)[1], 0)

    def kernel(
        series_ref, twiddle_ref, count_ref, target_ref, surface_ref, obs_ref, out_ref,
        series, per_cell, stage, recv, green, rows_scr, out_scr, press, recv2, surface_t_ref,
        load_sem, send_sem, recv_sem, send_sem2, recv_sem2,
    ):
        blk = lax.axis_index("blk")
        split = lax.axis_index("split")
        sub = lax.axis_index("sub")
        group = blk * n_split + split
        me = group * n_sub + sub

        def group_device(i):
            g = lax.rem(group + i, groups)
            return {"blk": g // n_split, "split": lax.rem(g, n_split), "sub": sub}

        def any_device(i):
            to = lax.rem(me + i, devices)
            g = to // n_sub
            return {"blk": g // n_split, "split": lax.rem(g, n_split), "sub": lax.rem(to, n_sub)}

        def total(ref, count):
            if count <= 16:
                return sum(ref[i].astype(jnp.float32) for i in range(count))
            zero = jnp.zeros(ref.shape[1:], jnp.float32)
            return lax.fori_loop(0, count, lambda i, s: s + ref[i].astype(jnp.float32), zero)

        def load(i):
            cells = pl.ds(i * chunk, chunk)
            return pltpu.make_async_copy(series_ref.at[cells], series.at[cells], load_sem.at[i])

        barrier = pltpu.get_barrier_semaphore()

        def greet(i):
            pl.semaphore_signal(barrier, inc=1, device_id=any_device(i), device_id_type=MESH)

        each(devices, greet)
        each(rows // chunk, lambda i: load(i).start(), 0)

        twiddle = jnp.concatenate([twiddle_ref[...]] * 8, axis=0)

        def transform(i):
            load(i).wait()
            records = pl.ds(pl.multiple_of(4 * i * chunk, 4 * chunk), 4 * chunk)
            per_cell[records, :] = lax.dot_general(
                series[pl.ds(i * chunk, chunk)].reshape(4 * chunk, samples),
                twiddle,
                (((1,), (1,)), ((), ())),
                preferred_element_type=jnp.float32,
            )

        each(rows // chunk, transform, 0)
        lane = lax.broadcasted_iota(jnp.int32, (rows, 128), 1)
        component = lane // (2 * NF) % 4
        spectrum = per_cell[pl.ds(0, rows, stride=4), :]
        for c in range(1, 4):
            spectrum = jnp.where(component == c, per_cell[pl.ds(c, rows, stride=4), :], spectrum)
        high = spectrum.astype(jnp.bfloat16).astype(jnp.float32)
        both = jnp.where(lane < 8 * NF, high, spectrum - high).T.astype(jnp.bfloat16)
        live = lax.broadcasted_iota(jnp.int32, (1, rows), 1) < count_ref[0]
        target = jnp.where(live, target_ref[...], -1)
        point = lax.broadcasted_iota(jnp.int32, (points, rows), 0)

        def partial_sums(g):
            chosen = (point == target - g * points).astype(jnp.float32).astype(jnp.bfloat16)
            sums = lax.dot_general(
                both, chosen, (((1,), (1,)), ((), ())), preferred_element_type=jnp.float32
            )
            return (sums[: 8 * NF] + sums[8 * NF :]).astype(jnp.bfloat16)

        def spectra_copy(i):
            return pltpu.make_async_remote_copy(
                src_ref=stage.at[i],
                dst_ref=recv.at[i],
                send_sem=send_sem.at[i],
                recv_sem=recv_sem.at[i],
                device_id=group_device(i),
                device_id_type=MESH,
            )

        pl.semaphore_wait(barrier, devices - 1)

        def send_spectra(i):
            stage[i] = partial_sums(lax.rem(group + i, groups))
            spectra_copy(i).start()

        each(groups, send_spectra)
        recv[0] = partial_sums(group)

        surface = surface_ref[...]
        surface_t_ref[...] = jnp.concatenate([surface, surface], axis=0).T

        def green_step(step, carry):
            start = pl.multiple_of(step * step_q, step_q)
            at = surface_t_ref[pl.ds(start, step_q), :]
            for h in range(n_obs // half):
                lanes = pl.ds(h * half, half)
                d_x = obs_ref[0:1, lanes] - at[:, 0:1]
                d_y = obs_ref[1:2, lanes] - at[:, 1:2]
                d_z = obs_ref[2:3, lanes] - at[:, 2:3]
                square = d_x * d_x + d_y * d_y + d_z * d_z
                inverse = lax.rsqrt(square)
                radius = square * inverse
                turns = radius * (0.25 / (2.0 * math.pi))
                turns = turns - jnp.round(turns)
                v = turns * turns
                cosine = horner(cos_c, v)
                sine = horner(sin_c, v) * turns
                twice = cosine + cosine
                scale = inverse * inverse
                old_r = cosine * scale
                old_i = -sine * scale
                new_r = twice * old_r - scale
                new_i = twice * old_i
                for f in range(NF):
                    k = 0.5 + 0.25 * f
                    base = f * 4 * points + start
                    parts = (
                        new_r * radius,
                        new_i * radius,
                        new_r * inverse - k * new_i,
                        new_i * inverse + k * new_r,
                    )
                    for p, value in enumerate(parts):
                        green[pl.ds(base + p * points, step_q), lanes] = value.astype(jnp.bfloat16)
                    old_r, new_r = new_r, twice * new_r - old_r
                    old_i, new_i = new_i, twice * new_i - old_i
            return carry

        lax.fori_loop(0, points // step_q, green_step, 0)

        each(groups, lambda i: spectra_copy(i).wait_recv())
        spectra = total(recv, groups)
        spectra = spectra * (surface[3:4] * (amplitude / (4.0 * math.pi)))
        wave = 0.5 + 0.25 * lax.broadcasted_iota(jnp.int32, (NF, points), 0).astype(jnp.float32)
        part = [
            (spectra[16 * c : 16 * c + NF], spectra[16 * c + NF : 16 * c + 2 * NF]) for c in range(4)
        ]
        mono_r = -wave * part[0][1]
        mono_i = wave * part[0][0]
        along_r = sum(surface[c : c + 1] * part[c + 1][0] for c in range(3))
        along_i = sum(surface[c : c + 1] * part[c + 1][1] for c in range(3))
        zero = jnp.zeros_like(wave)
        lines = [(mono_r, -mono_i, -along_r, along_i), (mono_i, mono_r, -along_i, -along_r)]
        for c in range(1, 4):
            r, i = part[c]
            lines.append((zero, zero, r, -i))
            lines.append((zero, zero, i, r))
        for t, line in enumerate(lines):
            for p, value in enumerate(line):
                for q in range(points // 128):
                    rows_scr[p * (points // 128) + q, t * NF : (t + 1) * NF, :] = value[
                        :, q * 128 : (q + 1) * 128
                    ]

        def radiate(f):
            left = jnp.concatenate(
                [rows_scr[p, pl.ds(f, 8, stride=NF), :] for p in range(4 * points // 128)], axis=1
            )
            left_high = left.astype(jnp.bfloat16).astype(jnp.float32)
            left = jnp.concatenate([left_high, left - left_high], axis=0).astype(jnp.bfloat16)
            result = jnp.dot(
                left,
                green[pl.ds(pl.multiple_of(f * 4 * points, 4 * points), 4 * points), :],
                preferred_element_type=jnp.float32,
            )
            result = result[:8] + result[8:]
            for q in range(n_obs // 128):
                out_scr[q, pl.ds(pl.multiple_of(f * 8, 8), 8), :] = result[:, q * 128 : (q + 1) * 128]

        each(NF, radiate, 0)
        for b in range(n_blk):
            for lane in range(b * obs_blk, (b + 1) * obs_blk, 128):
                lanes = slice(lane, lane + 128)
                terms = [out_scr[lane // 128, pl.ds(t, NF, stride=8), :] for t in range(8)]
                x, y, z = (obs_ref[c : c + 1, lanes] for c in range(3))
                inner = slice(lane - b * obs_blk, lane - b * obs_blk + 128)
                press[b, 0:NF, inner] = terms[0] + x * terms[2] + y * terms[4] + z * terms[6]
                press[b, NF : 2 * NF, inner] = terms[1] + x * terms[3] + y * terms[5] + z * terms[7]

        def pressure_copy(i):
            to = any_device(i)
            return pltpu.make_async_remote_copy(
                src_ref=press.at[to["blk"]],
                dst_ref=recv2.at[i],
                send_sem=send_sem2.at[i],
                recv_sem=recv_sem2.at[i],
                device_id=to,
                device_id_type=MESH,
            )

        each(devices, lambda i: pressure_copy(i).start())
        each(groups, lambda i: spectra_copy(i).wait_send())
        each(devices, lambda i: pressure_copy(i).wait_recv())
        recv2[0] = press[blk]
        out_ref[...] = total(recv2, devices)
        each(devices, lambda i: pressure_copy(i).wait_send())

    scratch = [
        pltpu.VMEM((rows, 4, samples), jnp.bfloat16),
        pltpu.VMEM((4 * rows, 128), jnp.float32),
        pltpu.VMEM((groups, 8 * NF, points), jnp.bfloat16),
        pltpu.VMEM((groups, 8 * NF, points), jnp.bfloat16),
        pltpu.VMEM((NF * 4 * points, n_obs), jnp.bfloat16),
        pltpu.VMEM((4 * points // 128, 8 * NF, 128), jnp.float32),
        pltpu.VMEM((n_obs // 128, 8 * NF, 128), jnp.float32),
        pltpu.VMEM((n_blk, 2 * NF, obs_blk), jnp.float32),
        pltpu.VMEM((devices, 2 * NF, obs_blk), jnp.float32),
        pltpu.VMEM((points, 8), jnp.float32),
        pltpu.SemaphoreType.DMA((rows // chunk,)),
        pltpu.SemaphoreType.DMA((groups,)),
        pltpu.SemaphoreType.DMA((groups,)),
        pltpu.SemaphoreType.DMA((devices,)),
        pltpu.SemaphoreType.DMA((devices,)),
    ]
    vmem = pl.BlockSpec(memory_space=pltpu.VMEM)
    return pl.pallas_call(
        kernel,
        out_shape=jax.ShapeDtypeStruct((2 * NF, obs_blk), jnp.float32),
        in_specs=[pl.BlockSpec(memory_space=pl.ANY), vmem, pl.BlockSpec(memory_space=pltpu.SMEM), vmem, vmem, vmem],
        out_specs=vmem,
        scratch_shapes=scratch,
        compiler_params=pltpu.CompilerParams(
            collective_id=0, has_side_effects=True, vmem_limit_bytes=56 * 2**20
        ),
    )


def local(cell_series, cell_count, cell_target, surface, observers):
    rows_dev, _, signal_readings = cell_series.shape
    points_dev = surface.shape[1]
    n_blk, n_split, n_sub = (lax.axis_size(a) for a in ("blk", "split", "sub"))
    devices = n_blk * n_split * n_sub
    amplitude = 150.0 * math.sqrt(
        signal_readings * points_dev / (rows_dev * (points_dev * devices))
    )
    twiddle = spectral_lookup_matrix(signal_readings)
    kernel = make_kernel(n_blk, n_split, n_sub, rows_dev, signal_readings, points_dev, observers.shape[1], amplitude)
    pressure = kernel(
        cell_series,
        twiddle,
        cell_count,
        cell_target.reshape(1, rows_dev),
        surface,
        observers,
    )
    return pressure.T.reshape(observers.shape[1] // n_blk, 2, NF)


def solution(mesh):
    return jax.shard_map(
        local,
        mesh=mesh,
        in_specs=(
            P(("case", "blk", "split", "sub"), None, None),
            P(("case", "blk", "split", "sub")),
            P(("case", "blk", "split", "sub")),
            P(None, ("case", "blk", "split", "sub")),
            P(None, "case"),
        ),
        out_specs=P(("case", "blk"), None, None),
        check_vma=False,
    )
```

```python
import math

import jax
import jax.numpy as jnp
import ml_dtypes
import numpy as np
from jax import lax
from jax.experimental import pallas as pl
from jax.experimental.pallas import tpu as pltpu
from jax.sharding import PartitionSpec as P

NF = 8
MESH = pl.DeviceIdType.MESH


def polynomials(terms):
    nodes = np.cos((np.arange(400) + 0.5) * np.pi / 400)
    squares = (nodes + 1.0) * 0.125
    u = np.sqrt(squares)
    out = []
    for values in (np.sin(2 * np.pi * u) / u, np.cos(2 * np.pi * u)):
        series = np.polynomial.chebyshev.chebfit(nodes, values, terms - 1)
        powers = np.polynomial.chebyshev.cheb2poly(series)
        total = np.zeros(1)
        for a in powers[::-1]:
            total = np.polynomial.polynomial.polyadd(
                np.polynomial.polynomial.polymul(total, [-1.0, 8.0]), [a]
            )
        out.append([float(np.float32(c)) for c in total[:terms]])
    return out


def spectral_lookup_matrix(signal_readings):
    moments = np.arange(signal_readings, dtype=np.int64)
    slots = np.arange(NF, dtype=np.int64) + signal_readings // 16
    modulo = slots[:, None] * moments[None, :] % signal_readings
    step = np.float32(2.0 * math.pi / signal_readings)
    phases = step * modulo.astype(np.float32)
    hann = np.float32(0.5) - np.float32(0.5) * np.cos(step * moments.astype(np.float32))
    scaled = np.float32(2.0 / signal_readings) * hann[None, :]
    table = np.concatenate([scaled * np.cos(phases), -scaled * np.sin(phases)], axis=0)
    return jnp.asarray(table.astype(ml_dtypes.bfloat16))


def horner(coefficients, v):
    total = coefficients[-1] * v + coefficients[-2]
    for c in coefficients[-3::-1]:
        total = total * v + c
    return total


def make_kernel(n_blk, n_split, n_sub, rows, samples, points, n_obs, amplitude):
    chunk = 128
    groups = n_blk * n_split
    devices = groups * n_sub
    obs_blk = n_obs // n_blk
    sin_c, cos_c = polynomials(7)
    half = 256 if n_obs % 256 == 0 else n_obs
    step_q = 16

    def each(count, body, first=1):
        lax.fori_loop(first, count, lambda i, c: (body(i), c)[1], 0)

    def kernel(
        series_ref, twiddle_ref, count_ref, target_ref, surface_ref, obs_ref, out_ref,
        series, per_cell, stage, recv, green, rows_scr, out_scr, press, recv2, surface_t_ref,
        load_sem, send_sem, recv_sem, send_sem2, recv_sem2,
    ):
        blk = lax.axis_index("blk")
        split = lax.axis_index("split")
        sub = lax.axis_index("sub")
        group = blk * n_split + split
        me = group * n_sub + sub

        def group_device(i):
            g = lax.rem(group + i, groups)
            return {"blk": g // n_split, "split": lax.rem(g, n_split), "sub": sub}

        def any_device(i):
            to = lax.rem(me + i, devices)
            g = to // n_sub
            return {"blk": g // n_split, "split": lax.rem(g, n_split), "sub": lax.rem(to, n_sub)}

        def total(ref, count):
            if count <= 16:
                return sum(ref[i].astype(jnp.float32) for i in range(count))
            zero = jnp.zeros(ref.shape[1:], jnp.float32)
            return lax.fori_loop(0, count, lambda i, s: s + ref[i].astype(jnp.float32), zero)

        def load(i):
            cells = pl.ds(i * chunk, chunk)
            return pltpu.make_async_copy(series_ref.at[cells], series.at[cells], load_sem.at[i])

        barrier = pltpu.get_barrier_semaphore()

        def greet(i):
            pl.semaphore_signal(barrier, inc=1, device_id=any_device(i), device_id_type=MESH)

        each(devices, greet)
        each(rows // chunk, lambda i: load(i).start(), 0)

        twiddle = jnp.concatenate([twiddle_ref[...]] * 8, axis=0)

        def transform(i):
            load(i).wait()
            records = pl.ds(pl.multiple_of(4 * i * chunk, 4 * chunk), 4 * chunk)
            per_cell[records, :] = lax.dot_general(
                series[pl.ds(i * chunk, chunk)].reshape(4 * chunk, samples),
                twiddle,
                (((1,), (1,)), ((), ())),
                preferred_element_type=jnp.float32,
            )

        each(rows // chunk, transform, 0)
        lane = lax.broadcasted_iota(jnp.int32, (rows, 128), 1)
        component = lane // (2 * NF) % 4
        spectrum = per_cell[pl.ds(0, rows, stride=4), :]
        for c in range(1, 4):
            spectrum = jnp.where(component == c, per_cell[pl.ds(c, rows, stride=4), :], spectrum)
        high = spectrum.astype(jnp.bfloat16).astype(jnp.float32)
        both = jnp.where(lane < 8 * NF, high, spectrum - high).T.astype(jnp.bfloat16)
        live = lax.broadcasted_iota(jnp.int32, (1, rows), 1) < count_ref[0]
        target = jnp.where(live, target_ref[...], -1)
        point = lax.broadcasted_iota(jnp.int32, (points, rows), 0)

        def partial_sums(g):
            chosen = (point == target - g * points).astype(jnp.float32).astype(jnp.bfloat16)
            sums = lax.dot_general(
                both, chosen, (((1,), (1,)), ((), ())), preferred_element_type=jnp.float32
            )
            return (sums[: 8 * NF] + sums[8 * NF :]).astype(jnp.bfloat16)

        def spectra_copy(i):
            return pltpu.make_async_remote_copy(
                src_ref=stage.at[i],
                dst_ref=recv.at[i],
                send_sem=send_sem.at[i],
                recv_sem=recv_sem.at[i],
                device_id=group_device(i),
                device_id_type=MESH,
            )


        def far_first(n, count):
            return count // 2 + (n // 2) * (2 * lax.rem(n, 2) - 1)

        def fill(i):
            stage[i] = partial_sums(lax.rem(group + i, groups))

        each(groups, fill)
        recv[0] = partial_sums(group)
        pl.semaphore_wait(barrier, devices - 1)
        each(groups, lambda n: spectra_copy(far_first(n, groups)).start())

        surface = surface_ref[...]
        surface_t_ref[...] = jnp.concatenate([surface, surface], axis=0).T

        def green_step(step, carry):
            start = pl.multiple_of(step * step_q, step_q)
            at = surface_t_ref[pl.ds(start, step_q), :]
            for h in range(n_obs // half):
                lanes = pl.ds(h * half, half)
                d_x = obs_ref[0:1, lanes] - at[:, 0:1]
                d_y = obs_ref[1:2, lanes] - at[:, 1:2]
                d_z = obs_ref[2:3, lanes] - at[:, 2:3]
                square = d_x * d_x + d_y * d_y + d_z * d_z
                inverse = lax.rsqrt(square)
                radius = square * inverse
                turns = radius * (0.25 / (2.0 * math.pi))
                turns = turns - jnp.round(turns)
                v = turns * turns
                cosine = horner(cos_c, v)
                sine = horner(sin_c, v) * turns
                twice = cosine + cosine
                scale = inverse * inverse
                old_r = cosine * scale
                old_i = -sine * scale
                new_r = twice * old_r - scale
                new_i = twice * old_i
                for f in range(NF):
                    k = 0.5 + 0.25 * f
                    base = f * 4 * points + start
                    parts = (
                        new_r * radius,
                        new_i * radius,
                        new_r * inverse - k * new_i,
                        new_i * inverse + k * new_r,
                    )
                    for p, value in enumerate(parts):
                        green[pl.ds(base + p * points, step_q), lanes] = value.astype(jnp.bfloat16)
                    old_r, new_r = new_r, twice * new_r - old_r
                    old_i, new_i = new_i, twice * new_i - old_i
            return carry

        lax.fori_loop(0, points // step_q, green_step, 0)

        each(groups, lambda i: spectra_copy(i).wait_recv())
        spectra = total(recv, groups)
        spectra = spectra * (surface[3:4] * (amplitude / (4.0 * math.pi)))
        wave = 0.5 + 0.25 * lax.broadcasted_iota(jnp.int32, (NF, points), 0).astype(jnp.float32)
        part = [
            (spectra[16 * c : 16 * c + NF], spectra[16 * c + NF : 16 * c + 2 * NF]) for c in range(4)
        ]
        mono_r = -wave * part[0][1]
        mono_i = wave * part[0][0]
        along_r = sum(surface[c : c + 1] * part[c + 1][0] for c in range(3))
        along_i = sum(surface[c : c + 1] * part[c + 1][1] for c in range(3))
        zero = jnp.zeros_like(wave)
        lines = [(mono_r, -mono_i, -along_r, along_i), (mono_i, mono_r, -along_i, -along_r)]
        for c in range(1, 4):
            r, i = part[c]
            lines.append((zero, zero, r, -i))
            lines.append((zero, zero, i, r))
        for t, line in enumerate(lines):
            for p, value in enumerate(line):
                for q in range(points // 128):
                    rows_scr[p * (points // 128) + q, t * NF : (t + 1) * NF, :] = value[
                        :, q * 128 : (q + 1) * 128
                    ]

        def radiate(f):
            left = jnp.concatenate(
                [rows_scr[p, pl.ds(f, 8, stride=NF), :] for p in range(4 * points // 128)], axis=1
            )
            left_high = left.astype(jnp.bfloat16).astype(jnp.float32)
            left = jnp.concatenate([left_high, left - left_high], axis=0).astype(jnp.bfloat16)
            result = jnp.dot(
                left,
                green[pl.ds(pl.multiple_of(f * 4 * points, 4 * points), 4 * points), :],
                preferred_element_type=jnp.float32,
            )
            result = result[:8] + result[8:]
            for q in range(n_obs // 128):
                out_scr[q, pl.ds(pl.multiple_of(f * 8, 8), 8), :] = result[:, q * 128 : (q + 1) * 128]

        each(NF, radiate, 0)
        for b in range(n_blk):
            for lane in range(b * obs_blk, (b + 1) * obs_blk, 128):
                lanes = slice(lane, lane + 128)
                terms = [out_scr[lane // 128, pl.ds(t, NF, stride=8), :] for t in range(8)]
                x, y, z = (obs_ref[c : c + 1, lanes] for c in range(3))
                inner = slice(lane - b * obs_blk, lane - b * obs_blk + 128)
                press[b, 0:NF, inner] = terms[0] + x * terms[2] + y * terms[4] + z * terms[6]
                press[b, NF : 2 * NF, inner] = terms[1] + x * terms[3] + y * terms[5] + z * terms[7]

        def pressure_copy(i):
            to = any_device(i)
            return pltpu.make_async_remote_copy(
                src_ref=press.at[to["blk"]],
                dst_ref=recv2.at[i],
                send_sem=send_sem2.at[i],
                recv_sem=recv_sem2.at[i],
                device_id=to,
                device_id_type=MESH,
            )

        each(devices, lambda n: pressure_copy(far_first(n, devices)).start())
        each(groups, lambda i: spectra_copy(i).wait_send())
        each(devices, lambda i: pressure_copy(i).wait_recv())
        recv2[0] = press[blk]
        out_ref[...] = total(recv2, devices)
        each(devices, lambda i: pressure_copy(i).wait_send())

    scratch = [
        pltpu.VMEM((rows, 4, samples), jnp.bfloat16),
        pltpu.VMEM((4 * rows, 128), jnp.float32),
        pltpu.VMEM((groups, 8 * NF, points), jnp.bfloat16),
        pltpu.VMEM((groups, 8 * NF, points), jnp.bfloat16),
        pltpu.VMEM((NF * 4 * points, n_obs), jnp.bfloat16),
        pltpu.VMEM((4 * points // 128, 8 * NF, 128), jnp.float32),
        pltpu.VMEM((n_obs // 128, 8 * NF, 128), jnp.float32),
        pltpu.VMEM((n_blk, 2 * NF, obs_blk), jnp.float32),
        pltpu.VMEM((devices, 2 * NF, obs_blk), jnp.float32),
        pltpu.VMEM((points, 8), jnp.float32),
        pltpu.SemaphoreType.DMA((rows // chunk,)),
        pltpu.SemaphoreType.DMA((groups,)),
        pltpu.SemaphoreType.DMA((groups,)),
        pltpu.SemaphoreType.DMA((devices,)),
        pltpu.SemaphoreType.DMA((devices,)),
    ]
    vmem = pl.BlockSpec(memory_space=pltpu.VMEM)
    return pl.pallas_call(
        kernel,
        out_shape=jax.ShapeDtypeStruct((2 * NF, obs_blk), jnp.float32),
        in_specs=[pl.BlockSpec(memory_space=pl.ANY), vmem, pl.BlockSpec(memory_space=pltpu.SMEM), vmem, vmem, vmem],
        out_specs=vmem,
        scratch_shapes=scratch,
        compiler_params=pltpu.CompilerParams(
            collective_id=0, has_side_effects=True, vmem_limit_bytes=56 * 2**20
        ),
    )


def local(cell_series, cell_count, cell_target, surface, observers):
    rows_dev, _, signal_readings = cell_series.shape
    points_dev = surface.shape[1]
    n_blk, n_split, n_sub = (lax.axis_size(a) for a in ("blk", "split", "sub"))
    devices = n_blk * n_split * n_sub
    amplitude = 150.0 * math.sqrt(
        signal_readings * points_dev / (rows_dev * (points_dev * devices))
    )
    twiddle = spectral_lookup_matrix(signal_readings)
    kernel = make_kernel(n_blk, n_split, n_sub, rows_dev, signal_readings, points_dev, observers.shape[1], amplitude)
    pressure = kernel(
        cell_series,
        twiddle,
        cell_count,
        cell_target.reshape(1, rows_dev),
        surface,
        observers,
    )
    return pressure.T.reshape(observers.shape[1] // n_blk, 2, NF)


def solution(mesh):
    return jax.shard_map(
        local,
        mesh=mesh,
        in_specs=(
            P(("case", "blk", "split", "sub"), None, None),
            P(("case", "blk", "split", "sub")),
            P(("case", "blk", "split", "sub")),
            P(None, ("case", "blk", "split", "sub")),
            P(None, "case"),
        ),
        out_specs=P(("case", "blk"), None, None),
        check_vma=False,
    )
```
